256 devices in a mesh: rcv: 32 (over z, x_lo, core), src: 8 (over x_hi, y).
Axes of the slice: x: 4 (x_hi: 2, x_lo: 2; x = x_hi * 2 + x_lo), y: 4, z: 8, core: 2. Of those that a mesh axis runs over, the one named last changes fastest.
Arguments:
- traces: bfloat16 [2, 2, 4096, 8192], P(None, None, 'rcv', 'src')
- tile_table: int32 [32, 17, 2], replicated, may hold values from 0 to 31, as said below
Outputs:
- psf_tiles: float32 [32, 17, 2, 2, 128, 128], P('rcv', None, None, None, 'src')
The draws below stay inside these ranges and needn't reach their ends.
Inputs may be any that keep to these rules, and one draw needn't show every extreme that they name: `tile_table`: each entry names a row block and a column block, the row block never past the column block; every such pair of the 32 blocks appears in some slot, and over all 544 slots no pair appears more than twice.
All inputs are finite; a program needn't handle non-finite values.
Results may differ from the reference program's by a relative error of at most 0.0003.
Values may be sent and summed in bfloat16 or wider, within the bound.
No kernel may reach another device: no remote copies, remote signals or barrier semaphores. Data moves between devices by JAX's collectives and lax.ppermute only.
A program may use at most 256 MiB of HBM per device.

```python
import jax
import jax.numpy as jnp
from jax import lax

R = 4096
S = 8192
NB = 32
BR = 128
K = 17
NT = 528


def draw_traces(key, part):
    key = jax.random.fold_in(key, 1)
    key_noise, key_scale = jax.random.split(key, 2)
    noise = jax.random.normal(key_noise, (2, 2, R, S), jnp.float32)
    scales = jnp.exp(jax.random.uniform(key_scale, (R,), jnp.float32, jnp.log(0.5), jnp.log(3.0)))
    values = scales[None, None, :, None] * noise / jnp.sqrt(jnp.float32(S))
    return values.astype(jnp.bfloat16)


def draw_tile_table(key, part):
    key = jax.random.fold_in(key, 2)
    order = jax.random.permutation(key, NB * K).astype(jnp.int32)
    tile_ids = jnp.where(order < NT, order, order - NT)
    blocks = jnp.arange(NB, dtype=jnp.int32)
    starts = blocks * NB - blocks * (blocks - 1) // 2
    row_ids = jnp.sum((starts[None, 1:] <= tile_ids[:, None]).astype(jnp.int32), axis=1)
    row_start = row_ids * NB - row_ids * (row_ids - 1) // 2
    col_ids = row_ids + tile_ids - row_start
    return jnp.stack([row_ids, col_ids], axis=1).reshape(NB, K, 2).astype(jnp.int32)


def setup_inputs(seed: int = 0) -> dict:
    seeds = jax.random.split(jax.random.key(seed), 3)
    traces = draw_traces(jax.random.fold_in(seeds[2], 71), 0)
    tile_table = draw_tile_table(jax.random.fold_in(seeds[2], 71), 0)
    return dict(traces=traces, tile_table=tile_table)


def tile_of(traces, pair):
    row_block = lax.dynamic_slice_in_dim(traces, (pair[0] * BR).astype(jnp.int32), BR, 2).astype(jnp.float32)
    col_block = lax.dynamic_slice_in_dim(traces, (pair[1] * BR).astype(jnp.int32), BR, 2).astype(jnp.float32)
    real_part = jnp.einsum("frs,fts->frt", row_block[:, 0], col_block[:, 0]) + jnp.einsum("frs,fts->frt", row_block[:, 1], col_block[:, 1])
    imag_part = jnp.einsum("frs,fts->frt", row_block[:, 1], col_block[:, 0]) - jnp.einsum("frs,fts->frt", row_block[:, 0], col_block[:, 1])
    return jnp.stack([real_part, imag_part], axis=1)


def reference(traces, tile_table):
    pairs = tile_table.reshape(NB * K, 2)
    tiles = lax.map(lambda pair: tile_of(traces, pair), pairs)
    return tiles.reshape(NB, K, 2, 2, BR, BR)
```

```python
import jax
import jax.numpy as jnp
from jax import lax
from jax.experimental import pallas as pl
from jax.experimental.pallas import tpu as pltpu
from jax.sharding import Mesh
from jax.sharding import PartitionSpec as P

NZ, NXL, NC, NXH, NY = 8, 2, 2, 2, 4
NX = NXH * NXL
K = 17
BR = 128
HS = 512
SLOTS = NZ * NXL * NC
X_AXIS = ("xl", "xh")


def rank(i, axis):
    return (i % NXL) * NXH + i // NXL if axis == X_AXIS else i


def shift(x, axis, size, step):
    return lax.ppermute(x, axis, [(rank(i, axis), rank((i + step) % size, axis)) for i in range(size)])


def swap(x, axis):
    return shift(x, axis, 2, 1)


def gather_chunks(own, other):
    mine = {}
    a, b = own, swap(other, "xl")
    mine[0, 0], mine[0, 1] = a, b
    af = ab = a
    bf = bb = b
    for k in range(1, 5):
        af = mine[(-k) % NZ, 0] = shift(af, "z", NZ, 1)
        if k < 4:
            ab = mine[k, 0] = shift(ab, "z", NZ, -1)
            bf = mine[(-k) % NZ, 1] = shift(bf, "z", NZ, 1)
        bb = mine[k, 1] = shift(bb, "z", NZ, -1)
    chunks = {}
    for (dz, xr), v in mine.items():
        chunks[dz, xr, 0] = v
        chunks[dz, xr, 1] = swap(v, "c")
    return [chunks[dz, xr, cr] for dz in range(NZ) for xr in range(NXL) for cr in range(NC)]


def tiles_kernel(slots, pos, *refs):
    chunks, rest = refs[:SLOTS], refs[SLOTS:]
    re_out, im_out = rest[0:5], rest[5:10]
    xs, gs, sem = rest[10:]
    copies = [pltpu.make_async_copy(chunks[i], xs.at[i], sem) for i in range(SLOTS)]
    for c in copies:
        c.start()
    for c in copies:
        c.wait()
    px = pos[0]
    py = pos[1]

    def put(outs, d1, d2, h, j, v):
        if d1 == 2:
            outs[2 + d2 // 2][d2 % 2, h, j] = v
        else:
            outs[{0: 0, 1: 1, 3: 4}[d1]][d2, h, j] = v

    for xr in range(NXL):
        groups = {}
        for dx in (xr, xr + 2):
            for dy in range(NY):
                xd = (px + dx) % NX
                groups[dx, dy] = pl.multiple_of(((xd // 2) * NY + (py + dy) % NY) * 16, 16)

        def tile(j, carry, xr=xr, groups=groups):
            t = xr * K + j
            u = xs[slots[2 * t]].reshape(2 * BR, HS)
            v = xs[slots[2 * t + 1]].reshape(2 * BR, HS)
            gs[...] = lax.dot_general(u, v, (((1,), (1,)), ((), ())), preferred_element_type=jnp.float32)
            for (dx, dy), row in groups.items():
                for h in range(2):
                    top = pl.ds(pl.multiple_of(row + h * 8, 8), 8)
                    low = pl.ds(pl.multiple_of(row + BR + h * 8, 8), 8)
                    put(re_out, dx, dy, h, j, gs[top, :BR] + gs[low, BR:])
                    put(im_out, dy, dx, h, j, gs[low, :BR] - gs[top, BR:])
            return carry

        lax.fori_loop(0, K, tile, 0)


def tile_partials(slots, pos, chunks):
    def part(n):
        return jax.ShapeDtypeStruct((n, 2, K, 8, BR), jnp.float32)

    sizes = [4, 4, 2, 2, 4] * 2
    smem = pl.BlockSpec(memory_space=pltpu.SMEM)
    outs = pl.pallas_call(
        tiles_kernel,
        out_shape=[part(n) for n in sizes],
        in_specs=[smem, smem] + [pl.BlockSpec(memory_space=pl.ANY)] * SLOTS,
        out_specs=[pl.BlockSpec(memory_space=pltpu.VMEM)] * len(sizes),
        scratch_shapes=[
            pltpu.VMEM((SLOTS, 2, BR, HS), jnp.bfloat16),
            pltpu.VMEM((2 * BR, 2 * BR), jnp.float32),
            pltpu.SemaphoreType.DMA,
        ],
        compiler_params=pltpu.CompilerParams(vmem_limit_bytes=15 * 1024 * 1024),
        cost_estimate=pl.CostEstimate(flops=2 * 34 * 256 * 256 * 512, bytes_accessed=13_000_000, transcendentals=0),
    )(slots, pos, *chunks)
    return outs[:5], outs[5:]


def reduce_ring2(parts, axis1, n1, axis2, n2):
    m0, m1, m2a, m2b, m3 = parts
    ra = shift(m2a, axis1, n1, 1)
    rb = shift(m2b, axis1, n1, -1)
    up = jnp.concatenate([m1[:2] + ra, m1[2:]], 0)
    down = jnp.concatenate([m3[:2], m3[2:] + rb], 0)
    ru = shift(up, axis1, n1, 1)
    rd = shift(down, axis1, n1, -1)
    t = m0 + ru + rd
    ra = shift(t[2, :1], axis2, n2, 1)
    rb = shift(t[2, 1:], axis2, n2, -1)
    up = jnp.concatenate([t[1, :1] + ra, t[1, 1:]], 0)
    down = jnp.concatenate([t[3, :1], t[3, 1:] + rb], 0)
    ru = shift(up, axis2, n2, 1)
    rd = shift(down, axis2, n2, -1)
    return t[0] + ru + rd


def body(traces, tile_table):
    z, xl, c = lax.axis_index("z"), lax.axis_index("xl"), lax.axis_index("c")
    px = lax.axis_index("xh") * NXL + xl
    py = lax.axis_index("y")
    pos = jnp.stack([px, py]).astype(jnp.int32)
    table = tile_table.reshape(NZ, NXL, NC, K, 2)
    mine = table[z, :, c]
    mine = jnp.where(xl == 0, mine, mine[::-1])
    slots = ((mine // 4 - z) % NZ) * 4 + ((mine // 2) % 2 ^ xl) * 2 + (mine % 2 ^ c)
    slots = slots.astype(jnp.int32).reshape(-1)

    own = lax.dynamic_slice_in_dim(traces, xl * HS, HS, 3)
    other = lax.dynamic_slice_in_dim(traces, (1 - xl) * HS, HS, 3)

    results = []
    for f in range(2):
        chunks = gather_chunks(own[f], other[f])
        re_parts, im_parts = tile_partials(slots, pos, chunks)
        re_sum = reduce_ring2(re_parts, X_AXIS, NX, "y", NY)
        im_sum = reduce_ring2(im_parts, "y", NY, X_AXIS, NX)
        results.append(jnp.stack([re_sum, im_sum]))
    out = jnp.stack(results)
    return out.transpose(3, 0, 1, 2, 4, 5).reshape(1, K, 2, 2, 16, BR)


def solution(mesh):
    axes = ("z", "xl", "c", "xh", "y")
    fine = Mesh(mesh.devices.reshape(NZ, NXL, NC, NXH, NY), axes)
    rcv, src = axes[:3], axes[3:]
    return jax.shard_map(
        body,
        mesh=fine,
        in_specs=(P(None, None, rcv, src), P()),
        out_specs=P(rcv, None, None, None, src, None),
        check_vma=False,
    )
```

```python
import jax
import jax.numpy as jnp
from jax import lax
from jax.experimental import pallas as pl
from jax.experimental.pallas import tpu as pltpu
from jax.sharding import Mesh
from jax.sharding import PartitionSpec as P

NZ, NXL, NC, NXH, NY = 8, 2, 2, 2, 4
NX = NXH * NXL
K = 17
BR = 128
HS = 512
X_AXIS = ("xl", "xh")


def rank(i, axis):
    return (i % NXL) * NXH + i // NXL if axis == X_AXIS else i


def shift(x, axis, size, step):
    return lax.ppermute(x, axis, [(rank(i, axis), rank((i + step) % size, axis)) for i in range(size)])


def swap(x, axis):
    return shift(x, axis, 2, 1)


def hbm_spec():
    return pl.BlockSpec(memory_space=pltpu.HBM)


def in_hbm(arrays):
    return [pltpu.with_memory_space_constraint(a, pltpu.HBM) for a in arrays]


def packed(arrays, after=()):
    n, m = len(arrays), len(after)

    def kernel(*refs):
        srcs, out, sem = refs[:n], refs[n + m], refs[-1]
        moves = [pltpu.make_async_copy(src, out.at[i], sem.at[i]) for i, src in enumerate(srcs)]
        for move in moves:
            move.start()
        for move in moves:
            move.wait()

    return pl.pallas_call(
        kernel,
        out_shape=pltpu.HBM((n,) + arrays[0].shape, arrays[0].dtype),
        in_specs=[pl.BlockSpec(memory_space=pltpu.VMEM)] * n + [pl.BlockSpec(memory_space=pl.ANY)] * m,
        out_specs=hbm_spec(),
        scratch_shapes=[pltpu.SemaphoreType.DMA((n,))],
        compiler_params=pltpu.CompilerParams(vmem_limit_bytes=8 * 1024 * 1024),
        cost_estimate=pl.CostEstimate(flops=0, bytes_accessed=4 * n * arrays[0].size, transcendentals=0),
    )(*arrays, *in_hbm(after))


def ring_step(a, b, k):
    (au, ad), (bu, bd) = a, b
    au = shift(au, "z", NZ, 1)
    ad = shift(ad, "z", NZ, -1) if k < 4 else None
    bu = shift(bu, "z", NZ, 1) if k < 4 else None
    bd = shift(bd, "z", NZ, -1)
    return (au, ad), (bu, bd)


def ring_gather(a, b):
    mine = packed([a, b])
    blocks = [(mine, (i,), (0, 0, i)) for i in range(2)]
    far = swap(mine, "c")
    blocks += [(far, (i,), (0, 1, i)) for i in range(2)]
    ra, rb = (a, a), (b, b)
    late = []
    for k in range(1, 5):
        ra, rb = ring_step(ra, rb, k)
        if k < 4:
            mine = packed([*ra, *rb])
            far = swap(mine, "c")
            late.append(far)
            for i, (dz, xr) in enumerate([(-k % NZ, 0), (k, 0), (-k % NZ, 1), (k, 1)]):
                blocks.append((mine, (i,), (dz, 0, xr)))
                blocks.append((far, (i,), (dz, 1, xr)))
        if k == 3:
            late = late[:2] + [mine]
    mine = packed([ra[0], rb[1]])
    far = swap(mine, "c")
    for i in range(2):
        blocks.append((mine, (i,), (4, 0, i)))
        blocks.append((far, (i,), (4, 1, i)))
    return blocks, late


def tile_partials(slots, pos, pairs, after=()):
    arrays = list({id(a): a for a, _, _ in pairs}.values())
    moves = [([a is x for x in arrays].index(True), src, dst) for a, src, dst in pairs]
    n, m = len(arrays), len(after)
    parts = [jax.ShapeDtypeStruct((NY, K, 16, BR), jnp.float32)] * (2 * NX)

    def kernel(slots, pos, *refs):
        chunks, outs = refs[:n], refs[n + m : n + m + len(parts)]
        xs, gs, sem = refs[n + m + len(parts) :]
        re_out, im_out = outs[:NX], outs[NX:]
        loads = [
            pltpu.make_async_copy(chunks[a].at[src], xs.at[dst], sem.at[i]) for i, (a, src, dst) in enumerate(moves)
        ]
        for load in loads:
            load.start()
        for load in loads:
            load.wait()
        px, py = pos[0], pos[1]
        rows = {}
        for dx in range(NX):
            for dy in range(NY):
                rows[dx, dy] = (((px + dx) % NX // 2) * NY + (py + dy) % NY) * 16

        def block(s):
            return xs[s // 4, (s // 2) % 2, s % 2].reshape(2 * BR, HS)

        def tile(j, buf, xr):
            t = xr * K + j
            u = block(slots[2 * t])
            v = block(slots[2 * t + 1])
            gs[buf] = lax.dot_general(u, v, (((1,), (1,)), ((), ())), preferred_element_type=jnp.float32)
            for dx in (xr, xr + 2):
                for dy in range(NY):
                    top = pl.ds(pl.multiple_of(rows[dx, dy], 16), 16)
                    low = pl.ds(pl.multiple_of(rows[dx, dy] + BR, 16), 16)
                    re_out[dx][dy, j] = gs[buf, top, :BR] + gs[buf, low, BR:]
                    im_out[dy][dx, j] = gs[buf, low, :BR] - gs[buf, top, BR:]

        for j in range(K):
            for xr in range(NXL):
                tile(j, (2 * j + xr) % 4, xr)

    smem = pl.BlockSpec(memory_space=pltpu.SMEM)
    outs = pl.pallas_call(
        kernel,
        out_shape=parts,
        in_specs=[smem, smem] + [pl.BlockSpec(memory_space=pl.ANY)] * (n + m),
        out_specs=[pl.BlockSpec(memory_space=pltpu.VMEM)] * len(parts),
        scratch_shapes=[
            pltpu.VMEM((NZ, NC, NXL, 2, BR, HS), jnp.bfloat16),
            pltpu.VMEM((4, 2 * BR, 2 * BR), jnp.float32),
            pltpu.SemaphoreType.DMA((len(pairs),)),
        ],
        compiler_params=pltpu.CompilerParams(vmem_limit_bytes=24 * 1024 * 1024),
        cost_estimate=pl.CostEstimate(flops=2 * 34 * 256 * 256 * 512, bytes_accessed=13_000_000, transcendentals=0),
    )(slots.reshape(-1), pos, *in_hbm(arrays), *after)
    return outs[:NX], outs[NX:]


def reduce_far(parts, axis):
    got = [parts[0]] + [shift(parts[d], axis, NX, d) for d in (2, 1, 3)]
    return [got[0][d] + got[1][d] + got[2][d] + got[3][d] for d in range(NY)]


def reduce_near(sums, axis):
    both = [jnp.stack([f[d] for f in sums], 1) for d in range(NY)]
    got = [both[0]] + [shift(both[d], axis, NY, d) for d in (2, 1, 3)]
    return got[0] + got[1] + got[2] + got[3]


def body(traces, tile_table):
    z, xl, c = lax.axis_index("z"), lax.axis_index("xl"), lax.axis_index("c")
    px = lax.axis_index("xh") * NXL + xl
    py = lax.axis_index("y")
    pos = jnp.stack([px, py]).astype(jnp.int32)
    mine = tile_table.reshape(NZ, NXL, NC, K, 2)[z, :, c]
    mine = jnp.where(xl == 0, mine, mine[::-1])
    near = (mine // 2) % 2 ^ xl
    slots_rel = (((mine // 4 - z) % NZ) * 4 + (mine % 2 ^ c) * 2 + near).astype(jnp.int32)
    slots_abs = ((mine // 4) * 4 + (mine % 2) * 2 + near).astype(jnp.int32)

    own = lax.dynamic_slice_in_dim(traces, xl * HS, HS, 3)
    other = lax.dynamic_slice_in_dim(traces, (1 - xl) * HS, HS, 3)

    blocks, late = ring_gather(own[0], swap(other[0], "xl"))
    both = packed([own[1], swap(other[1], "xl")], after=late)
    whole = lax.all_gather(both, ("z", "c")).reshape(NZ, NC, NXL, 2, BR, HS)

    re_parts, im_parts = tile_partials(slots_rel, pos, blocks, after=in_hbm([both]))
    re_first, im_first = reduce_far(re_parts, X_AXIS), reduce_far(im_parts, "y")

    blocks = [(whole, (dz,), (dz,)) for dz in range(NZ)]
    re_parts, im_parts = tile_partials(slots_abs, pos, blocks, after=(*re_first, *im_first))
    re_second, im_second = reduce_far(re_parts, X_AXIS), reduce_far(im_parts, "y")
    re_sum = reduce_near((re_first, re_second), "y")
    im_sum = reduce_near((im_first, im_second), X_AXIS)
    return jnp.stack([re_sum, im_sum], 2)[None]


def solution(mesh):
    axes = ("z", "xl", "c", "xh", "y")
    fine = Mesh(mesh.devices.reshape(NZ, NXL, NC, NXH, NY), axes)
    rcv, src = axes[:3], axes[3:]
    return jax.shard_map(
        body,
        mesh=fine,
        in_specs=(P(None, None, rcv, src), P()),
        out_specs=P(rcv, None, None, None, src, None),
        check_vma=False,
    )
```

```python
import jax
import jax.numpy as jnp
from jax import lax
from jax.experimental import pallas as pl
from jax.experimental.pallas import tpu as pltpu
from jax.sharding import Mesh
from jax.sharding import PartitionSpec as P

NZ, NXL, NC, NXH, NY = 8, 2, 2, 2, 4
NX = NXH * NXL
K = 17
BR = 128
HS = 512
X_AXIS = ("xl", "xh")


def rank(i, axis):
    return (i % NXL) * NXH + i // NXL if axis == X_AXIS else i


def shift(x, axis, size, step):
    return lax.ppermute(x, axis, [(rank(i, axis), rank((i + step) % size, axis)) for i in range(size)])


def swap(x, axis):
    return shift(x, axis, 2, 1)


def hbm_spec():
    return pl.BlockSpec(memory_space=pltpu.HBM)


def in_hbm(arrays):
    return [pltpu.with_memory_space_constraint(a, pltpu.HBM) for a in arrays]


def packed(arrays, after=()):
    n, m = len(arrays), len(after)

    def kernel(*refs):
        srcs, out, sem = refs[:n], refs[n + m], refs[-1]
        moves = [pltpu.make_async_copy(src, out.at[i], sem.at[i]) for i, src in enumerate(srcs)]
        for move in moves:
            move.start()
        for move in moves:
            move.wait()

    return pl.pallas_call(
        kernel,
        out_shape=pltpu.HBM((n,) + arrays[0].shape, arrays[0].dtype),
        in_specs=[pl.BlockSpec(memory_space=pltpu.VMEM)] * n + [pl.BlockSpec(memory_space=pl.ANY)] * m,
        out_specs=hbm_spec(),
        scratch_shapes=[pltpu.SemaphoreType.DMA((n,))],
        compiler_params=pltpu.CompilerParams(vmem_limit_bytes=8 * 1024 * 1024),
        cost_estimate=pl.CostEstimate(flops=0, bytes_accessed=16_000_000, transcendentals=0),
    )(*arrays, *after)


def ring_step(a, b, k):
    (au, ad), (bu, bd) = a, b
    au = shift(au, "z", NZ, 1)
    ad = shift(ad, "z", NZ, -1) if k < 4 else None
    bu = shift(bu, "z", NZ, 1) if k < 4 else None
    bd = shift(bd, "z", NZ, -1)
    return (au, ad), (bu, bd)


def place(dz, xrel, crel):
    k = jnp.minimum(dz, NZ - dz)
    inner = 4 * k - 2 + 2 * xrel + (dz < 4)
    return crel * (NZ * NXL) + jnp.where(dz == 0, xrel, jnp.where(dz == 4, 14 + xrel, inner))


def ring_gather(a, b):
    near = [packed([a, b])]
    ra, rb = (a, a), (b, b)
    for k in range(1, 4):
        ra, rb = ring_step(ra, rb, k)
        if k < 3:
            near.append(packed([*ra, *rb]))
    late = [*in_hbm(near), *ra, *rb]
    new = list(ra + rb)
    ra, rb = ring_step(ra, rb, 4)
    near.append(packed([*new, ra[0], rb[1]]))
    return near + [swap(v, "c") for v in near], late


def tile_partials(slots, pos, stacks, after=()):
    n, m = len(stacks), len(after)
    starts = [sum(a.shape[0] for a in stacks[:i]) for i in range(n)]
    parts = [jax.ShapeDtypeStruct((n2, K, 16, BR), jnp.float32) for n2 in [NY] * NX + [NX] * 3 + [NX // 2] * 2]

    def kernel(slots, pos, *refs):
        chunks, outs = refs[:n], refs[n + m : n + m + len(parts)]
        xs, gs, sem = refs[n + m + len(parts) :]
        re_out = outs[:NX]
        im_home, im_up, im_down, im_keep_up, im_keep_down = outs[NX:]

        def put_im(dy, dx, j, v):
            low = dx < 2
            if dy == 0:
                im_home[dx, j] = v
            elif dy == 2:
                (im_up if low else im_down)[dx % 2, j] = v
            elif dy == 1:
                (im_keep_up if low else im_up)[dx, j] = v
            elif low:
                im_down[dx + 2, j] = v
            else:
                im_keep_down[dx - 2, j] = v

        loads = [
            pltpu.make_async_copy(chunks[i], xs.at[pl.ds(starts[i], stacks[i].shape[0])], sem.at[i]) for i in range(n)
        ]
        for load in loads:
            load.start()
        for load in loads:
            load.wait()
        px, py = pos[0], pos[1]
        rows = {}
        for dx in range(NX):
            for dy in range(NY):
                rows[dx, dy] = (((px + dx) % NX // 2) * NY + (py + dy) % NY) * 16

        def block(s):
            return xs[s].reshape(2 * BR, HS)

        def tile(j, buf, xr):
            t = xr * K + j
            u = block(slots[2 * t])
            v = block(slots[2 * t + 1])
            gs[buf] = lax.dot_general(u, v, (((1,), (1,)), ((), ())), preferred_element_type=jnp.float32)
            for dx in (xr, xr + 2):
                for dy in range(NY):
                    top = pl.ds(pl.multiple_of(rows[dx, dy], 16), 16)
                    low = pl.ds(pl.multiple_of(rows[dx, dy] + BR, 16), 16)
                    re_out[dx][dy, j] = gs[buf, top, :BR] + gs[buf, low, BR:]
                    put_im(dy, dx, j, gs[buf, low, :BR] - gs[buf, top, BR:])

        for j in range(K):
            for xr in range(NXL):
                tile(j, (2 * j + xr) % 4, xr)

    smem = pl.BlockSpec(memory_space=pltpu.SMEM)
    outs = pl.pallas_call(
        kernel,
        out_shape=parts,
        in_specs=[smem, smem] + [pl.BlockSpec(memory_space=pl.ANY)] * (n + m),
        out_specs=[pl.BlockSpec(memory_space=pltpu.VMEM)] * len(parts),
        scratch_shapes=[
            pltpu.VMEM((NZ * NC * NXL, 2, BR, HS), jnp.bfloat16),
            pltpu.VMEM((4, 2 * BR, 2 * BR), jnp.float32),
            pltpu.SemaphoreType.DMA((n,)),
        ],
        compiler_params=pltpu.CompilerParams(vmem_limit_bytes=24 * 1024 * 1024),
        cost_estimate=pl.CostEstimate(flops=2 * 34 * 256 * 256 * 512, bytes_accessed=13_000_000, transcendentals=0),
    )(slots.reshape(-1), pos, *in_hbm(stacks), *after)
    return outs[:NX], outs[NX:]


def reduce_far(re_parts, im_parts):
    home, up, down, keep_up, keep_down = im_parts
    got = [re_parts[0]] + [shift(re_parts[d], X_AXIS, NX, d) for d in (1, 3, 2)]
    up, down = shift(up, "y", NY, 1), shift(down, "y", NY, -1)
    last_up = shift(keep_up + up[:2], "y", NY, 1)
    last_down = shift(keep_down + down[:2], "y", NY, -1)
    re_sums = [got[0][d] + got[1][d] + got[2][d] + got[3][d] for d in range(NY)]
    im_sums = [home[d] + down[2 + d] + last_up[d] for d in range(2)]
    im_sums += [home[d] + up[d] + last_down[d - 2] for d in range(2, NX)]
    return re_sums, im_sums, [*got[1:], last_up, last_down]


def reduce_near(sums, axis):
    both = [jnp.stack([f[d] for f in sums], 1) for d in range(NY)]
    got = [both[0]] + [shift(both[d], axis, NY, d) for d in (2, 1, 3)]
    return got[0] + got[1] + got[2] + got[3]


def body(traces, tile_table):
    z, xl, c = lax.axis_index("z"), lax.axis_index("xl"), lax.axis_index("c")
    px = lax.axis_index("xh") * NXL + xl
    py = lax.axis_index("y")
    pos = jnp.stack([px, py]).astype(jnp.int32)
    mine = tile_table.reshape(NZ, NXL, NC, K, 2)[z, :, c]
    mine = jnp.where(xl == 0, mine, mine[::-1])
    near = (mine // 2) % 2 ^ xl
    slots_rel = place((mine // 4 - z) % NZ, near, mine % 2 ^ c).astype(jnp.int32)
    slots_abs = ((mine // 4) * 4 + (mine % 2) * 2 + near).astype(jnp.int32)

    own = lax.dynamic_slice_in_dim(traces, xl * HS, HS, 3)
    other = lax.dynamic_slice_in_dim(traces, (1 - xl) * HS, HS, 3)

    stacks, late = ring_gather(own[0], swap(other[0], "xl"))
    both = packed([own[1], swap(other[1], "xl")], after=late)
    whole = lax.all_gather(both, ("z", "c"), tiled=True)

    re_parts, im_parts = tile_partials(slots_rel, pos, stacks, after=in_hbm([both]))
    re_first, im_first, come = reduce_far(re_parts, im_parts)

    re_parts, im_parts = tile_partials(slots_abs, pos, [whole], after=in_hbm(come))
    re_second, im_second, _ = reduce_far(re_parts, im_parts)
    re_sum = reduce_near((re_first, re_second), "y")
    im_sum = reduce_near((im_first, im_second), X_AXIS)
    return jnp.stack([re_sum, im_sum], 2)[None]


def solution(mesh):
    axes = ("z", "xl", "c", "xh", "y")
    fine = Mesh(mesh.devices.reshape(NZ, NXL, NC, NXH, NY), axes)
    rcv, src = axes[:3], axes[3:]
    return jax.shard_map(
        body,
        mesh=fine,
        in_specs=(P(None, None, rcv, src), P()),
        out_specs=P(rcv, None, None, None, src, None),
        check_vma=False,
    )
```

```python
import jax
import jax.numpy as jnp
from jax import lax
from jax.experimental import pallas as pl
from jax.experimental.pallas import tpu as pltpu
from jax.sharding import Mesh
from jax.sharding import PartitionSpec as P

NZ, NXL, NC, NXH, NY = 8, 2, 2, 2, 4
NX = NXH * NXL
K = 17
BR = 128
HS = 512
X_AXIS = ("xl", "xh")


def rank(i, axis):
    return (i % NXL) * NXH + i // NXL if axis == X_AXIS else i


def shift(x, axis, size, step):
    return lax.ppermute(x, axis, [(rank(i, axis), rank((i + step) % size, axis)) for i in range(size)])


def swap(x, axis):
    return shift(x, axis, 2, 1)


def hbm_spec():
    return pl.BlockSpec(memory_space=pltpu.HBM)


def in_hbm(arrays):
    return [pltpu.with_memory_space_constraint(a, pltpu.HBM) for a in arrays]


def packed(arrays, after=()):
    n, m = len(arrays), len(after)

    def kernel(*refs):
        srcs, out, sem = refs[:n], refs[n + m], refs[-1]
        moves = [pltpu.make_async_copy(src, out.at[i], sem.at[i]) for i, src in enumerate(srcs)]
        for move in moves:
            move.start()
        for move in moves:
            move.wait()

    return pl.pallas_call(
        kernel,
        out_shape=pltpu.HBM((n,) + arrays[0].shape, arrays[0].dtype),
        in_specs=[pl.BlockSpec(memory_space=pltpu.VMEM)] * n + [pl.BlockSpec(memory_space=pl.ANY)] * m,
        out_specs=hbm_spec(),
        scratch_shapes=[pltpu.SemaphoreType.DMA((n,))],
        compiler_params=pltpu.CompilerParams(vmem_limit_bytes=8 * 1024 * 1024),
        cost_estimate=pl.CostEstimate(flops=0, bytes_accessed=16_000_000, transcendentals=0),
    )(*arrays, *after)


def ring_step(a, b, k):
    (au, ad), (bu, bd) = a, b
    au = shift(au, "z", NZ, 1)
    ad = shift(ad, "z", NZ, -1) if k < 4 else None
    bu = shift(bu, "z", NZ, 1) if k < 4 else None
    bd = shift(bd, "z", NZ, -1)
    return (au, ad), (bu, bd)


def place(dz, xrel, crel):
    k = jnp.minimum(dz, NZ - dz)
    inner = 4 * k - 2 + 2 * xrel + (dz < 4)
    return crel * (NZ * NXL) + jnp.where(dz == 0, xrel, jnp.where(dz == 4, 14 + xrel, inner))


def ring_gather(a, b):
    near = [packed([a, b])]
    ra, rb = (a, a), (b, b)
    for k in range(1, 4):
        ra, rb = ring_step(ra, rb, k)
        if k < 3:
            near.append(packed([*ra, *rb]))
    late = [*in_hbm(near), *ra, *rb]
    new = list(ra + rb)
    ra, rb = ring_step(ra, rb, 4)
    near.append(packed([*new, ra[0], rb[1]]))
    return near + [swap(v, "c") for v in near], late


def tile_partials(slots, pos, stacks, direct, after=()):
    n, m = len(stacks), len(after)
    starts = [sum(a.shape[0] for a in stacks[:i]) for i in range(n)]
    ring_sizes = [NX] * 3 + [NX // 2] * 2
    re_sizes = [NY] * NX if direct else ring_sizes
    parts = [jax.ShapeDtypeStruct((n2, K, 16, BR), jnp.float32) for n2 in re_sizes + ring_sizes]

    def kernel(slots, pos, *refs):
        chunks, outs = refs[:n], refs[n + m : n + m + len(parts)]
        xs, sem = refs[n + m + len(parts) :]
        re_out, im_out = outs[: len(re_sizes)], outs[len(re_sizes) :]

        def put(refs, d1, d2, j, v):
            if len(refs) == NX:
                refs[d1][d2, j] = v
                return
            home, up, down, keep_up, keep_down = refs
            low = d2 < 2
            if d1 == 0:
                home[d2, j] = v
            elif d1 == 2:
                (up if low else down)[d2 % 2, j] = v
            elif d1 == 1:
                (keep_up if low else up)[d2, j] = v
            elif low:
                down[d2 + 2, j] = v
            else:
                keep_down[d2 - 2, j] = v

        loads = [
            pltpu.make_async_copy(chunks[i], xs.at[pl.ds(starts[i], stacks[i].shape[0])], sem.at[i]) for i in range(n)
        ]
        for load in loads:
            load.start()
        for load in loads:
            load.wait()
        px, py = pos[0], pos[1]
        rows = {}
        for dx in range(NX):
            for dy in range(NY):
                rows[dx, dy] = (((px + dx) % NX // 2) * NY + (py + dy) % NY) * 16

        def tile(j, xr):
            t = xr * K + j
            row_block, col_block = slots[2 * t], slots[2 * t + 1]
            groups = [(dx, dy) for dx in (xr, xr + 2) for dy in range(NY)]
            u = [xs[row_block, part, pl.ds(pl.multiple_of(rows[g], 16), 16)] for part in range(2) for g in groups]
            v = xs[col_block].reshape(2 * BR, HS)
            g = lax.dot_general(
                jnp.concatenate(u, 0), v, (((1,), (1,)), ((), ())), preferred_element_type=jnp.float32
            )
            re_tile = g[:BR, :BR] + g[BR:, BR:]
            im_tile = g[BR:, :BR] - g[:BR, BR:]
            for i, (dx, dy) in enumerate(groups):
                put(re_out, dx, dy, j, re_tile[i * 16 : (i + 1) * 16])
                put(im_out, dy, dx, j, im_tile[i * 16 : (i + 1) * 16])

        for j in range(K):
            for xr in range(NXL):
                tile(j, xr)

    smem = pl.BlockSpec(memory_space=pltpu.SMEM)
    outs = pl.pallas_call(
        kernel,
        out_shape=parts,
        in_specs=[smem, smem] + [pl.BlockSpec(memory_space=pl.ANY)] * (n + m),
        out_specs=[pl.BlockSpec(memory_space=pltpu.VMEM)] * len(parts),
        scratch_shapes=[
            pltpu.VMEM((NZ * NC * NXL, 2, BR, HS), jnp.bfloat16),
            pltpu.SemaphoreType.DMA((n,)),
        ],
        compiler_params=pltpu.CompilerParams(vmem_limit_bytes=24 * 1024 * 1024),
        cost_estimate=pl.CostEstimate(flops=2 * 34 * 256 * 256 * 512, bytes_accessed=13_000_000, transcendentals=0),
    )(slots.reshape(-1), pos, *in_hbm(stacks), *after)
    return outs[: len(re_sizes)], outs[len(re_sizes) :]


def reduce_direct(parts, axis):
    got = [parts[0]] + [shift(parts[d], axis, NX, d) for d in (1, 3, 2)]
    return [got[0][d] + got[1][d] + got[2][d] + got[3][d] for d in range(NY)], got[1:]


def reduce_ring(parts, axis):
    home, up, down, keep_up, keep_down = parts
    up, down = shift(up, axis, NX, 1), shift(down, axis, NX, -1)
    last_up = shift(keep_up + up[:2], axis, NX, 1)
    last_down = shift(keep_down + down[:2], axis, NX, -1)
    sums = [home[d] + down[2 + d] + last_up[d] for d in range(2)]
    sums += [home[d] + up[d] + last_down[d - 2] for d in range(2, NX)]
    return sums, [last_up, last_down]


def reduce_near(sums, axis):
    both = [jnp.stack([f[d] for f in sums], 1) for d in range(NY)]
    got = [both[0]] + [shift(both[d], axis, NY, d) for d in (2, 1, 3)]
    return got[0] + got[1] + got[2] + got[3]


def body(traces, tile_table):
    z, xl, c = lax.axis_index("z"), lax.axis_index("xl"), lax.axis_index("c")
    px = lax.axis_index("xh") * NXL + xl
    py = lax.axis_index("y")
    pos = jnp.stack([px, py]).astype(jnp.int32)
    mine = tile_table.reshape(NZ, NXL, NC, K, 2)[z, :, c]
    mine = jnp.where(xl == 0, mine, mine[::-1])
    near = (mine // 2) % 2 ^ xl
    slots_rel = place((mine // 4 - z) % NZ, near, mine % 2 ^ c).astype(jnp.int32)
    slots_abs = ((mine // 4) * 4 + (mine % 2) * 2 + near).astype(jnp.int32)

    own = lax.dynamic_slice_in_dim(traces, xl * HS, HS, 3)
    other = lax.dynamic_slice_in_dim(traces, (1 - xl) * HS, HS, 3)

    stacks, late = ring_gather(own[0], swap(other[0], "xl"))
    both = packed([own[1], swap(other[1], "xl")], after=late)
    whole = lax.all_gather(both, ("z", "c"), tiled=True)

    re_parts, im_parts = tile_partials(slots_rel, pos, stacks, True, after=in_hbm([both]))
    re_first, re_come = reduce_direct(re_parts, X_AXIS)
    im_first, _ = reduce_ring(im_parts, "y")

    re_parts, im_parts = tile_partials(slots_abs, pos, [whole], False, after=[*in_hbm(re_come), *im_first])
    re_second, _ = reduce_ring(re_parts, X_AXIS)
    im_second, _ = reduce_ring(im_parts, "y")
    re_sum = reduce_near((re_first, re_second), "y")
    im_sum = reduce_near((im_first, im_second), X_AXIS)
    return jnp.stack([re_sum, im_sum], 2)[None]


def solution(mesh):
    axes = ("z", "xl", "c", "xh", "y")
    fine = Mesh(mesh.devices.reshape(NZ, NXL, NC, NXH, NY), axes)
    rcv, src = axes[:3], axes[3:]
    return jax.shard_map(
        body,
        mesh=fine,
        in_specs=(P(None, None, rcv, src), P()),
        out_specs=P(rcv, None, None, None, src, None),
        check_vma=False,
    )
```

```python
import jax
import jax.numpy as jnp
from jax import lax
from jax.experimental import pallas as pl
from jax.experimental.pallas import tpu as pltpu
from jax.sharding import Mesh
from jax.sharding import PartitionSpec as P

NZ, NXL, NC, NXH, NY = 8, 2, 2, 2, 4
NX = NXH * NXL
K = 17
BR = 128
HS = 512
X_AXIS = ("xl", "xh")


def rank(i, axis):
    return (i % NXL) * NXH + i // NXL if axis == X_AXIS else i


def shift(x, axis, size, step):
    return lax.ppermute(x, axis, [(rank(i, axis), rank((i + step) % size, axis)) for i in range(size)])


def swap(x, axis):
    return shift(x, axis, 2, 1)


def hbm_spec():
    return pl.BlockSpec(memory_space=pltpu.HBM)


def in_hbm(arrays):
    return [pltpu.with_memory_space_constraint(a, pltpu.HBM) for a in arrays]


def packed(arrays, after=()):
    n, m = len(arrays), len(after)

    def kernel(*refs):
        srcs, out, sem = refs[:n], refs[n + m], refs[-1]
        moves = [pltpu.make_async_copy(src, out.at[i], sem.at[i]) for i, src in enumerate(srcs)]
        for move in moves:
            move.start()
        for move in moves:
            move.wait()

    return pl.pallas_call(
        kernel,
        out_shape=pltpu.HBM((n,) + arrays[0].shape, arrays[0].dtype),
        in_specs=[pl.BlockSpec(memory_space=pltpu.VMEM)] * n + [pl.BlockSpec(memory_space=pl.ANY)] * m,
        out_specs=hbm_spec(),
        scratch_shapes=[pltpu.SemaphoreType.DMA((n,))],
        compiler_params=pltpu.CompilerParams(vmem_limit_bytes=8 * 1024 * 1024),
        cost_estimate=pl.CostEstimate(flops=0, bytes_accessed=16_000_000, transcendentals=0),
    )(*arrays, *after)


def ring_step(a, b, k):
    (au, ad), (bu, bd) = a, b
    au = shift(au, "z", NZ, 1)
    ad = shift(ad, "z", NZ, -1) if k < 4 else None
    bu = shift(bu, "z", NZ, 1) if k < 4 else None
    bd = shift(bd, "z", NZ, -1)
    return (au, ad), (bu, bd)


def place(dz, xrel, crel):
    k = jnp.minimum(dz, NZ - dz)
    inner = 4 * k - 2 + 2 * xrel + (dz < 4)
    return crel * (NZ * NXL) + jnp.where(dz == 0, xrel, jnp.where(dz == 4, 14 + xrel, inner))


def ring_gather(a, b):
    near = [packed([a, b])]
    ra, rb = (a, a), (b, b)
    for k in range(1, 4):
        ra, rb = ring_step(ra, rb, k)
        if k < 3:
            near.append(packed([*ra, *rb]))
    late = [*in_hbm(near), *ra, *rb]
    new = list(ra + rb)
    ra, rb = ring_step(ra, rb, 4)
    near.append(packed([*new, ra[0], rb[1]]))
    return near + [swap(v, "c") for v in near], late


def tile_partials(slots, pos, stacks, direct, after=()):
    n, m = len(stacks), len(after)
    starts = [sum(a.shape[0] for a in stacks[:i]) for i in range(n)]
    ring_sizes = [NX] * 3 + [NX // 2] * 2
    re_sizes = [NY] * NX if direct else ring_sizes
    parts = [jax.ShapeDtypeStruct((n2, K, 16, BR), jnp.float32) for n2 in re_sizes + ring_sizes]

    def kernel(slots, pos, *refs):
        chunks, outs = refs[:n], refs[n + m : n + m + len(parts)]
        xs, sem = refs[n + m + len(parts) :]
        re_out, im_out = outs[: len(re_sizes)], outs[len(re_sizes) :]

        def put(refs, d1, d2, j, v):
            if len(refs) == NX:
                refs[d1][d2, j] = v
                return
            home, up, down, keep_up, keep_down = refs
            low = d2 < 2
            if d1 == 0:
                home[d2, j] = v
            elif d1 == 2:
                (up if low else down)[d2 % 2, j] = v
            elif d1 == 1:
                (keep_up if low else up)[d2, j] = v
            elif low:
                down[d2 + 2, j] = v
            else:
                keep_down[d2 - 2, j] = v

        loads = [
            pltpu.make_async_copy(chunks[i], xs.at[pl.ds(starts[i], stacks[i].shape[0])], sem.at[i]) for i in range(n)
        ]
        for load in loads:
            load.start()
        for load in loads:
            load.wait()
        px, py = pos[0], pos[1]
        rows = {}
        for dx in range(NX):
            for dy in range(NY):
                rows[dx, dy] = (((px + dx) % NX // 2) * NY + (py + dy) % NY) * 16

        def tile(j, xr):
            t = xr * K + j
            row_block, col_block = slots[2 * t], slots[2 * t + 1]
            groups = [(dx, dy) for dx in (xr, xr + 2) for dy in range(NY)]
            u = [xs[row_block, part, pl.ds(pl.multiple_of(rows[g], 16), 16)] for part in range(2) for g in groups]
            v = xs[col_block].reshape(2 * BR, HS)
            g = lax.dot_general(
                jnp.concatenate(u, 0), v, (((1,), (1,)), ((), ())), preferred_element_type=jnp.float32
            )
            re_tile = g[:BR, :BR] + g[BR:, BR:]
            im_tile = g[BR:, :BR] - g[:BR, BR:]
            for i, (dx, dy) in enumerate(groups):
                put(re_out, dx, dy, j, re_tile[i * 16 : (i + 1) * 16])
                put(im_out, dy, dx, j, im_tile[i * 16 : (i + 1) * 16])

        for j in range(K):
            for xr in range(NXL):
                tile(j, xr)

    smem = pl.BlockSpec(memory_space=pltpu.SMEM)
    outs = pl.pallas_call(
        kernel,
        out_shape=parts,
        in_specs=[smem, smem] + [pl.BlockSpec(memory_space=pl.ANY)] * (n + m),
        out_specs=[pl.BlockSpec(memory_space=pltpu.VMEM)] * len(parts),
        scratch_shapes=[
            pltpu.VMEM((NZ * NC * NXL, 2, BR, HS), jnp.bfloat16),
            pltpu.SemaphoreType.DMA((n,)),
        ],
        compiler_params=pltpu.CompilerParams(vmem_limit_bytes=24 * 1024 * 1024),
        cost_estimate=pl.CostEstimate(flops=2 * 34 * 256 * 256 * 512, bytes_accessed=13_000_000, transcendentals=0),
    )(slots.reshape(-1), pos, *in_hbm(stacks), *after)
    return outs[: len(re_sizes)], outs[len(re_sizes) :]


def reduce_direct(parts, axis):
    got = [parts[0]] + [shift(parts[d], axis, NX, d) for d in (1, 3, 2)]
    return [got[0][d] + got[1][d] + got[2][d] + got[3][d] for d in range(NY)], got[1:]


def reduce_ring(parts, axis):
    home, up, down, keep_up, keep_down = parts
    up, down = shift(up, axis, NX, 1), shift(down, axis, NX, -1)
    last_up = shift(keep_up + up[:2], axis, NX, 1)
    last_down = shift(keep_down + down[:2], axis, NX, -1)
    sums = [home[d] + down[2 + d] + last_up[d] for d in range(2)]
    sums += [home[d] + up[d] + last_down[d - 2] for d in range(2, NX)]
    return sums, [last_up, last_down]


def reduce_near(sums, axis):
    both = [jnp.stack([f[d] for f in sums], 1) for d in range(NY)]
    got = [both[0]] + [shift(both[d], axis, NY, d) for d in (2, 1, 3)]
    return got[0] + got[1] + got[2] + got[3]


def body(traces, tile_table):
    z, xl, c = lax.axis_index("z"), lax.axis_index("xl"), lax.axis_index("c")
    px = lax.axis_index("xh") * NXL + xl
    py = lax.axis_index("y")
    pos = jnp.stack([px, py]).astype(jnp.int32)
    mine = tile_table.reshape(NZ, NXL, NC, K, 2)[z, :, c]
    mine = jnp.where(xl == 0, mine, mine[::-1])
    near = (mine // 2) % 2 ^ xl
    slots_rel = place((mine // 4 - z) % NZ, near, mine % 2 ^ c).astype(jnp.int32)
    slots_abs = ((mine // 4) * 4 + (mine % 2) * 2 + near).astype(jnp.int32)

    own = lax.dynamic_slice_in_dim(traces, xl * HS, HS, 3)
    other = lax.dynamic_slice_in_dim(traces, (1 - xl) * HS, HS, 3)

    stacks, late = ring_gather(own[0], swap(other[0], "xl"))
    both = packed([own[1], swap(other[1], "xl")], after=late)
    whole = lax.all_gather(both, ("z", "c"), tiled=True)

    re_parts, im_parts = tile_partials(slots_rel, pos, stacks, True, after=in_hbm([both]))
    re_first, re_come = reduce_direct(re_parts, X_AXIS)
    im_first, _ = reduce_ring(im_parts, "y")

    re_parts, im_parts = tile_partials(slots_abs, pos, [whole], False, after=[*in_hbm(re_come), *im_first[2:]])
    re_second, _ = reduce_ring(re_parts, X_AXIS)
    im_second, _ = reduce_ring(im_parts, "y")
    re_sum = reduce_near((re_first, re_second), "y")
    im_sum = reduce_near((im_first, im_second), X_AXIS)
    return jnp.stack([re_sum, im_sum], 2)[None]


def solution(mesh):
    axes = ("z", "xl", "c", "xh", "y")
    fine = Mesh(mesh.devices.reshape(NZ, NXL, NC, NXH, NY), axes)
    rcv, src = axes[:3], axes[3:]
    return jax.shard_map(
        body,
        mesh=fine,
        in_specs=(P(None, None, rcv, src), P()),
        out_specs=P(rcv, None, None, None, src, None),
        check_vma=False,
    )
```

```python
import jax
import jax.numpy as jnp
from jax import lax
from jax.experimental import pallas as pl
from jax.experimental.pallas import tpu as pltpu
from jax.sharding import Mesh
from jax.sharding import PartitionSpec as P

NZ, NXL, NC, NXH, NY = 8, 2, 2, 2, 4
NX = NXH * NXL
K = 17
BR = 128
HS = 512
X_AXIS = ("xl", "xh")


def rank(i, axis):
    return (i % NXL) * NXH + i // NXL if axis == X_AXIS else i


def shift(x, axis, size, step):
    return lax.ppermute(x, axis, [(rank(i, axis), rank((i + step) % size, axis)) for i in range(size)])


def swap(x, axis):
    return shift(x, axis, 2, 1)


def hbm_spec():
    return pl.BlockSpec(memory_space=pltpu.HBM)


def in_hbm(arrays):
    return [pltpu.with_memory_space_constraint(a, pltpu.HBM) for a in arrays]


def packed(arrays, after=()):
    n, m = len(arrays), len(after)

    def kernel(*refs):
        srcs, out, sem = refs[:n], refs[n + m], refs[-1]
        moves = [pltpu.make_async_copy(src, out.at[i], sem.at[i]) for i, src in enumerate(srcs)]
        for move in moves:
            move.start()
        for move in moves:
            move.wait()

    return pl.pallas_call(
        kernel,
        out_shape=pltpu.HBM((n,) + arrays[0].shape, arrays[0].dtype),
        in_specs=[pl.BlockSpec(memory_space=pltpu.VMEM)] * n + [pl.BlockSpec(memory_space=pl.ANY)] * m,
        out_specs=hbm_spec(),
        scratch_shapes=[pltpu.SemaphoreType.DMA((n,))],
        compiler_params=pltpu.CompilerParams(vmem_limit_bytes=8 * 1024 * 1024),
        cost_estimate=pl.CostEstimate(flops=0, bytes_accessed=16_000_000, transcendentals=0),
    )(*arrays, *after)


def ring_step(a, b, k):
    (au, ad), (bu, bd) = a, b
    au = shift(au, "z", NZ, 1)
    ad = shift(ad, "z", NZ, -1) if k < 4 else None
    bu = shift(bu, "z", NZ, 1) if k < 4 else None
    bd = shift(bd, "z", NZ, -1)
    return (au, ad), (bu, bd)


def place(dz, xrel, crel):
    k = jnp.minimum(dz, NZ - dz)
    inner = 4 * k - 2 + 2 * xrel + (dz < 4)
    return crel * (NZ * NXL) + jnp.where(dz == 0, xrel, jnp.where(dz == 4, 14 + xrel, inner))


def ring_gather(a, b):
    near = [packed([a, b])]
    ra, rb = (a, a), (b, b)
    for k in range(1, 4):
        ra, rb = ring_step(ra, rb, k)
        if k < 3:
            near.append(packed([*ra, *rb]))
    late = [*in_hbm(near), *ra, *rb]
    new = list(ra + rb)
    ra, rb = ring_step(ra, rb, 4)
    near.append(packed([*new, ra[0], rb[1]]))
    return near + [swap(v, "c") for v in near], late


def tile_partials(slots, pos, stacks, direct, after=()):
    n, m = len(stacks), len(after)
    starts = [sum(a.shape[0] for a in stacks[:i]) for i in range(n)]
    ring_sizes = [NX] * 3 + [NX // 2] * 2
    re_sizes = [NY] * NX if direct else ring_sizes
    parts = [jax.ShapeDtypeStruct((n2, K, 16, BR), jnp.float32) for n2 in re_sizes + ring_sizes]

    def kernel(slots, pos, *refs):
        chunks, outs = refs[:n], refs[n + m : n + m + len(parts)]
        xs, sem = refs[n + m + len(parts) :]
        re_out, im_out = outs[: len(re_sizes)], outs[len(re_sizes) :]

        def put(refs, d1, d2, j, v):
            if len(refs) == NX:
                refs[d1][d2, j] = v
                return
            home, up, down, keep_up, keep_down = refs
            low = d2 < 2
            if d1 == 0:
                home[d2, j] = v
            elif d1 == 2:
                (up if low else down)[d2 % 2, j] = v
            elif d1 == 1:
                (keep_up if low else up)[d2, j] = v
            elif low:
                down[d2 + 2, j] = v
            else:
                keep_down[d2 - 2, j] = v

        loads = [
            pltpu.make_async_copy(chunks[i], xs.at[pl.ds(starts[i], stacks[i].shape[0])], sem.at[i]) for i in range(n)
        ]
        for load in loads:
            load.start()
        for load in loads:
            load.wait()
        px, py = pos[0], pos[1]
        rows = {}
        for dx in range(NX):
            for dy in range(NY):
                rows[dx, dy] = (((px + dx) % NX // 2) * NY + (py + dy) % NY) * 16

        def tile(j, xr):
            t = xr * K + j
            row_block, col_block = slots[2 * t], slots[2 * t + 1]
            groups = [(dx, dy) for dx in (xr, xr + 2) for dy in range(NY)]
            u = [xs[row_block, part, pl.ds(pl.multiple_of(rows[g], 16), 16)] for part in range(2) for g in groups]
            v = xs[col_block].reshape(2 * BR, HS)
            g = lax.dot_general(
                jnp.concatenate(u, 0), v, (((1,), (1,)), ((), ())), preferred_element_type=jnp.float32
            )
            re_tile = g[:BR, :BR] + g[BR:, BR:]
            im_tile = g[BR:, :BR] - g[:BR, BR:]
            for i, (dx, dy) in enumerate(groups):
                put(re_out, dx, dy, j, re_tile[i * 16 : (i + 1) * 16])
                put(im_out, dy, dx, j, im_tile[i * 16 : (i + 1) * 16])

        for j in range(K):
            for xr in range(NXL):
                tile(j, xr)

    smem = pl.BlockSpec(memory_space=pltpu.SMEM)
    outs = pl.pallas_call(
        kernel,
        out_shape=parts,
        in_specs=[smem, smem] + [pl.BlockSpec(memory_space=pl.ANY)] * (n + m),
        out_specs=[pl.BlockSpec(memory_space=pltpu.VMEM)] * len(parts),
        scratch_shapes=[
            pltpu.VMEM((NZ * NC * NXL, 2, BR, HS), jnp.bfloat16),
            pltpu.SemaphoreType.DMA((n,)),
        ],
        compiler_params=pltpu.CompilerParams(vmem_limit_bytes=24 * 1024 * 1024),
        cost_estimate=pl.CostEstimate(flops=2 * 34 * 256 * 256 * 512, bytes_accessed=13_000_000, transcendentals=0),
    )(slots.reshape(-1), pos, *in_hbm(stacks), *after)
    return outs[: len(re_sizes)], outs[len(re_sizes) :]


def reduce_direct(parts, axis):
    got = [parts[0]] + [shift(parts[d], axis, NX, d) for d in (1, 3, 2)]
    return [got[0][d] + got[1][d] + got[2][d] + got[3][d] for d in range(NY)], got[1:]


def reduce_ring(parts, axis):
    home, up, down, keep_up, keep_down = parts
    up, down = shift(up, axis, NX, 1), shift(down, axis, NX, -1)
    last_up = shift(keep_up + up[:2], axis, NX, 1)
    last_down = shift(keep_down + down[:2], axis, NX, -1)
    sums = [home[d] + down[2 + d] + last_up[d] for d in range(2)]
    sums += [home[d] + up[d] + last_down[d - 2] for d in range(2, NX)]
    return sums, [last_up, last_down]


def reduce_near(sums, axis):
    both = [jnp.stack([f[d] for f in sums], 1) for d in range(NY)]
    got = [both[0]] + [shift(both[d], axis, NY, d) for d in (2, 1, 3)]
    return got


def assemble(re_got, im_got):
    def kernel(*refs):
        out = refs[-1]
        for i, got in enumerate((refs[:NY], refs[NY : 2 * NY])):
            for j in range(K):
                for f in range(2):
                    out[0, j, f, i] = (got[0][j, f] + got[1][j, f]) + (got[2][j, f] + got[3][j, f])

    vmem = pl.BlockSpec(memory_space=pltpu.VMEM)
    return pl.pallas_call(
        kernel,
        out_shape=jax.ShapeDtypeStruct((1, K, 2, 2, 16, BR), jnp.float32),
        in_specs=[vmem] * (2 * NY),
        out_specs=vmem,
        compiler_params=pltpu.CompilerParams(vmem_limit_bytes=8 * 1024 * 1024),
        cost_estimate=pl.CostEstimate(flops=500_000, bytes_accessed=3_000_000, transcendentals=0),
    )(*re_got, *im_got)


def body(traces, tile_table):
    z, xl, c = lax.axis_index("z"), lax.axis_index("xl"), lax.axis_index("c")
    px = lax.axis_index("xh") * NXL + xl
    py = lax.axis_index("y")
    pos = jnp.stack([px, py]).astype(jnp.int32)
    mine = tile_table.reshape(NZ, NXL, NC, K, 2)[z, :, c]
    mine = jnp.where(xl == 0, mine, mine[::-1])
    near = (mine // 2) % 2 ^ xl
    slots_rel = place((mine // 4 - z) % NZ, near, mine % 2 ^ c).astype(jnp.int32)
    slots_abs = ((mine // 4) * 4 + (mine % 2) * 2 + near).astype(jnp.int32)

    own = lax.dynamic_slice_in_dim(traces, xl * HS, HS, 3)
    other = lax.dynamic_slice_in_dim(traces, (1 - xl) * HS, HS, 3)

    stacks, late = ring_gather(own[0], swap(other[0], "xl"))
    both = packed([own[1], swap(other[1], "xl")], after=late)
    whole = lax.all_gather(both, ("z", "c"), tiled=True)

    re_parts, im_parts = tile_partials(slots_rel, pos, stacks, True, after=in_hbm([both]))
    re_first, re_come = reduce_direct(re_parts, X_AXIS)
    im_first, _ = reduce_ring(im_parts, "y")

    re_parts, im_parts = tile_partials(slots_abs, pos, [whole], False, after=[*in_hbm(re_come), *im_first])
    re_second, _ = reduce_ring(re_parts, X_AXIS)
    im_second, _ = reduce_ring(im_parts, "y")
    re_got = reduce_near((re_first, re_second), "y")
    im_got = reduce_near((im_first, im_second), X_AXIS)
    return assemble(re_got, im_got)


def solution(mesh):
    axes = ("z", "xl", "c", "xh", "y")
    fine = Mesh(mesh.devices.reshape(NZ, NXL, NC, NXH, NY), axes)
    rcv, src = axes[:3], axes[3:]
    return jax.shard_map(
        body,
        mesh=fine,
        in_specs=(P(None, None, rcv, src), P()),
        out_specs=P(rcv, None, None, None, src, None),
        check_vma=False,
    )
```
